32 devices in a mesh: dp: 4 (over y, x), mp: 8 (over z, core).
Axes of the slice: x: 2, y: 2, z: 4, core: 2. Of those that a mesh axis runs over, the one named last changes fastest.
Arguments:
- activations: bfloat16 [2048, 4096], P('dp', 'mp'), may hold values from -22 to 22
- out_grads: bfloat16 [2048, 32768], P('dp', 'mp'), may hold values from -1 to 1
- weight: float32 [4096, 32768], P('dp', 'mp'), may hold values from -0.09375 to 0.09375
- row_state: float32 [4096], P('dp'), may hold values from 0.1 to 1.6
- column_state: float32 [32768], P('mp'), may hold values from 0.1 to 1.6
- next_batch: bfloat16 [2048, 4096], P('dp', 'mp'), may hold values from -6 to 6
Outputs:
- new_weight: float32 [4096, 32768], P('dp', 'mp')
- update: float32 [4096, 32768], P('dp', 'mp')
- row_moment: float32 [4096], P('dp')
- column_moment: float32 [32768], P('mp')
- next_hidden: bfloat16 [2048, 32768], P('dp', 'mp')
The draws below stay inside these ranges and needn't reach their ends.
All inputs are finite; a program needn't handle non-finite values.
Results may differ from the reference program's by a relative error of at most 0.001.
The reference program's roundings to bfloat16 on the way (of `weight_half`) count: a program that leaves them out, or rounds other values in their place, can miss the bound.
Values may be sent and summed in bfloat16 or wider, within the bound.
No kernel may reach another device: no remote copies, remote signals or barrier semaphores. Data moves between devices by JAX's collectives and lax.ppermute only.
A program may use at most 192 MiB of HBM per device.

```python
import math
import jax
import jax.numpy as jnp
from jax import lax

D = 4096
FF = 32768
TOKENS = 2048


def column_scales(key, number):
    place = jnp.arange(number, dtype=jnp.float32) / number
    spread = jax.random.uniform(key, (number,), jnp.float32, -0.5, 0.5)
    return 3.0 ** (place - 0.5) * 10.0 ** spread


def scaled_rows(key, width):
    keys = jax.random.split(key, 2)
    scales = column_scales(keys[0], width)
    values = jnp.clip(jax.random.normal(keys[1], (TOKENS, width), jnp.float32), -4.0, 4.0)
    return values * scales[None, :]


def draw_activations(key, part):
    values = scaled_rows(jax.random.fold_in(key, 11), D)
    return values.astype(jnp.bfloat16)


def draw_out_grads(key, part):
    values = scaled_rows(jax.random.fold_in(key, 23), FF)
    values = values / (3.0 * jnp.sqrt(jnp.float32(TOKENS)))
    return values.astype(jnp.bfloat16)


def block_levels(own_key, dims, cuts, low, high):
    level = 1.0
    for position, shards_of in cuts:
        steps = jax.random.uniform(jax.random.fold_in(jax.random.fold_in(own_key, 6), position), (shards_of,), jnp.float32, low / len(cuts), high / len(cuts))
        level = level * jnp.repeat(jnp.exp(steps), dims[position] // shards_of).reshape((-1,) + (1,) * (len(dims) - 1 - position))
    return level


def normal_values(stream_key, extent, deviation, limit, cuts=(), kind=jnp.bfloat16):
    result = deviation * jax.random.normal(stream_key, extent, jnp.float32)
    if cuts:
        result = result * block_levels(stream_key, extent, cuts, -0.22, 0.18)
    return jnp.clip(result, -limit, limit).astype(kind)


def setup_inputs(seed: int = 0) -> dict:
    arg_keys = jax.random.split(jax.random.key(seed), 7)
    activations = draw_activations(jax.random.fold_in(arg_keys[6], 71), 0)
    out_grads = draw_out_grads(jax.random.fold_in(arg_keys[6], 71), 0)
    weight = normal_values(arg_keys[2], (D, FF), D ** -0.5, 0.09375, ((0, 4), (1, 8)), jnp.float32)
    row_state = jnp.clip(jnp.exp(math.log(1.6) - 2.7725887 * jax.random.uniform(arg_keys[3], (D,), jnp.float32) ** block_levels(arg_keys[3], (D,), ((0, 4),), -0.2, 0.2)), 0.1, 1.6)
    column_state = jnp.clip(jnp.exp(math.log(1.6) - 2.7725887 * jax.random.uniform(arg_keys[4], (FF,), jnp.float32) ** block_levels(arg_keys[4], (FF,), ((0, 8),), -0.2, 0.2)), 0.1, 1.6)
    next_batch = normal_values(arg_keys[5], (TOKENS, D), 1.0, 6.0, ((0, 4), (1, 8)))
    return {"activations": activations, "out_grads": out_grads, "weight": weight, "row_state": row_state, "column_state": column_state, "next_batch": next_batch}


tiny_square = 1e-30
weight_eps = 1e-06
decay_rate = 0.5
clip_level = 0.5
learn_rate = 0.01

def reference(activations, out_grads, weight, row_state, column_state, next_batch):
    gradient = jnp.dot(activations.T, out_grads, preferred_element_type=jnp.float32)
    squares = gradient * gradient + tiny_square
    row_moment = decay_rate * row_state + (1.0 - decay_rate) * lax.optimization_barrier(jnp.mean(squares, axis=1))
    column_moment = decay_rate * column_state + (1.0 - decay_rate) * lax.optimization_barrier(jnp.mean(squares, axis=0))
    raw_update = gradient * lax.rsqrt(row_moment[:, None] * column_moment[None, :])
    rms_update = jnp.sqrt(jnp.mean(raw_update * raw_update))
    update = raw_update / jnp.maximum(1.0, rms_update / clip_level)
    rms_weight = jnp.sqrt(jnp.mean(weight * weight) + weight_eps)
    new_weight = weight - learn_rate * rms_weight * update
    weight_half = new_weight.astype(jnp.bfloat16)
    next_hidden = jnp.dot(next_batch, weight_half, preferred_element_type=jnp.float32).astype(jnp.bfloat16)
    return (new_weight, update, row_moment, column_moment, next_hidden)
```

```python
import functools

import jax
import jax.numpy as jnp
from jax import lax
from jax.experimental import pallas as pl
from jax.experimental.pallas import tpu as pltpu
from jax.sharding import PartitionSpec as P

tiny_square = 1e-30
weight_eps = 1e-06
decay_rate = 0.5
clip_level = 0.5
learn_rate = 0.01

f32, bf16 = jnp.float32, jnp.bfloat16
CHUNKS = 8
LANES = 128
SCALE_ROWS = 16
VMEM = 48 * 2**20
SPAN, BASE = 252.0, 125.5


def swap(value, axis, size, bits):
    return lax.ppermute(value, axis, [(i, i ^ bits) for i in range(size)])


def all_sum(value, axis, size):
    bit = 1
    while bit < size:
        value = value + swap(value, axis, size, bit)
        bit *= 2
    return value


def bit_order(dp, chunk):
    bits = [1 << n for n in range(dp.bit_length() - 1)]
    turn = chunk % len(bits)
    return bits[turn:] + bits[:turn]


def params(name=None):
    return pltpu.CompilerParams(vmem_limit_bytes=VMEM)


def encode(values):
    top = jnp.max(jnp.abs(values), axis=0, keepdims=True)
    top = jnp.maximum(top * 1.01, 1e-30).astype(bf16)
    part = jnp.sqrt(jnp.abs(values) * (1.0 / top.astype(f32)))
    size = jnp.exp2(part * SPAN - BASE)
    return jnp.where(values < 0, -size, size).astype(bf16), top


def decode(code, top):
    code = code.astype(f32)
    part = (jnp.log2(jnp.abs(code)) + BASE) * (1.0 / SPAN)
    size = part * part * top.astype(f32)
    return jnp.where(code < 0, -size, size)


def put_code(out_ref, values):
    rows = values.shape[0]
    code, top = encode(values)
    out_ref[0:rows, :] = code
    out_ref[rows : rows + SCALE_ROWS, :] = jnp.broadcast_to(top, (SCALE_ROWS, top.shape[1]))


def get_code(ref):
    rows = ref.shape[0] - SCALE_ROWS
    return decode(ref[0:rows, :], ref[rows : rows + 1, :])


def gradient_kernel(dp, first, *refs):
    left = refs[0]
    blocks = refs[1 : 1 + dp]
    gradient, rows, columns = refs[-3:]
    depth = blocks[0].shape[0]
    total = None
    for n in range(dp):
        part = jnp.dot(left[:, n * depth : (n + 1) * depth], blocks[n][...], preferred_element_type=f32)
        total = part if total is None else total + part
    gradient[...] = total
    squares = total * total + tiny_square
    columns[...] = jnp.sum(squares, axis=0, keepdims=True)
    lanes = squares[:, 0:LANES]
    for n in range(1, squares.shape[1] // LANES):
        lanes = lanes + squares[:, n * LANES : (n + 1) * LANES]

    @pl.when(pl.program_id(0) == 0)
    def _():
        rows[...] = lanes if first else refs[1 + dp][...] + lanes

    @pl.when(pl.program_id(0) > 0)
    def _():
        rows[...] += lanes


def gradient_chunk(left, own, others, before, chunk, width, tile):
    rows, tokens = left.shape
    depth, columns = own.shape
    dp = 1 + len(others)
    at = chunk * width // tile
    whole = lambda shape: pl.BlockSpec(shape, lambda j: (0, 0))
    in_specs = [whole(left.shape), pl.BlockSpec((depth, tile), lambda j: (0, at + j))]
    in_specs += [pl.BlockSpec((depth, tile), lambda j: (0, j))] * len(others)
    args = [left, own, *others]
    aliases = {}
    if before is not None:
        gradient, row_part, column_part = before
        aliases = {len(args) + 1: 0, len(args) + 2: 2}
        args += [row_part, gradient, column_part]
        in_specs += [whole((rows, LANES)), pl.BlockSpec(memory_space=pl.ANY), pl.BlockSpec(memory_space=pl.ANY)]
    return pl.pallas_call(
        functools.partial(gradient_kernel, dp, before is None),
        grid=(width // tile,),
        in_specs=in_specs,
        out_specs=[
            pl.BlockSpec((rows, tile), lambda j: (0, at + j)),
            whole((rows, LANES)),
            pl.BlockSpec((1, tile), lambda j: (0, at + j)),
        ],
        out_shape=[
            jax.ShapeDtypeStruct((rows, columns), f32),
            jax.ShapeDtypeStruct((rows, LANES), f32),
            jax.ShapeDtypeStruct((1, columns), f32),
        ],
        input_output_aliases=aliases,
        compiler_params=params(),
        cost_estimate=pl.CostEstimate(
            flops=2 * rows * tokens * width, bytes_accessed=4 * rows * width + 2 * tokens * (rows + width), transcendentals=0
        ),
        name="gradient_chunk",
    )(*args)


def raw_kernel(gradient, row_scale, column_scale, out):
    g = gradient[...]
    out[...] = jnp.sum(g * g * row_scale[...], axis=0, keepdims=True) * column_scale[...]


def raw_square_sum(gradient, row_scale, column_scale, tile):
    rows, columns = gradient.shape
    return pl.pallas_call(
        raw_kernel,
        grid=(columns // tile,),
        in_specs=[
            pl.BlockSpec((rows, tile), lambda j: (0, j)),
            pl.BlockSpec((rows, 1), lambda j: (0, 0)),
            pl.BlockSpec((1, tile), lambda j: (0, j)),
        ],
        out_specs=pl.BlockSpec((1, tile), lambda j: (0, j)),
        out_shape=jax.ShapeDtypeStruct((1, columns), f32),
        compiler_params=params(),
        cost_estimate=pl.CostEstimate(flops=4 * rows * columns, bytes_accessed=4 * rows * columns, transcendentals=0),
        name="raw_square_sum",
    )(gradient, row_scale, column_scale)


def update_kernel(order, depth, step, gradient, weight, row_scale, column_scale, features, *refs):
    new_weight, update, sent, kept = refs[-4:]
    change = gradient[...] * row_scale[...] * column_scale[...]
    update[...] = change
    fresh = weight[...] - step[0, 0] * change
    new_weight[...] = fresh
    half = fresh.astype(bf16)
    parts = [
        jnp.dot(features[n * depth : (n + 1) * depth, :], half, preferred_element_type=f32) for n in order
    ]
    middle = len(order) // 2
    for n in range(middle):
        kept[n * depth : (n + 1) * depth, :] = parts[n]
    put_code(sent, jnp.concatenate(parts[middle:], axis=0))


def update_chunk(gradient, weight, row_scale, column_scale, step, features, before, chunk, width, tile, order):
    rows, columns = gradient.shape
    tokens = features.shape[0]
    depth = tokens // len(order)
    at = chunk * width // tile
    block = pl.BlockSpec((rows, tile), lambda j: (0, at + j))
    args = [step, gradient, weight, row_scale, column_scale, features]
    in_specs = [
        pl.BlockSpec(memory_space=pltpu.SMEM),
        block,
        block,
        pl.BlockSpec((rows, 1), lambda j: (0, 0)),
        pl.BlockSpec((1, tile), lambda j: (0, at + j)),
        pl.BlockSpec(features.shape, lambda j: (0, 0)),
    ]
    aliases = {}
    if before is not None:
        aliases = {len(args): 0, len(args) + 1: 1}
        args += list(before)
        in_specs += [pl.BlockSpec(memory_space=pl.ANY)] * 2
    half = tokens // 2
    return pl.pallas_call(
        functools.partial(update_kernel, order, depth),
        grid=(width // tile,),
        in_specs=in_specs,
        out_specs=[
            block,
            block,
            pl.BlockSpec((half + SCALE_ROWS, tile), lambda j: (0, j)),
            pl.BlockSpec((half, tile), lambda j: (0, j)),
        ],
        out_shape=[
            jax.ShapeDtypeStruct((rows, columns), f32),
            jax.ShapeDtypeStruct((rows, columns), f32),
            jax.ShapeDtypeStruct((half + SCALE_ROWS, width), bf16),
            jax.ShapeDtypeStruct((half, width), f32),
        ],
        input_output_aliases=aliases,
        compiler_params=params(),
        cost_estimate=pl.CostEstimate(
            flops=2 * rows * tokens * width,
            bytes_accessed=16 * rows * width + 3 * tokens * width + 2 * tokens * rows,
            transcendentals=tokens * width,
        ),
        name="update_chunk",
    )(*args)


def fold_kernel(kept, arrived, sent, left):
    total = kept[...] + get_code(arrived)
    half = total.shape[0] // 2
    left[...] = total[0:half, :]
    put_code(sent, total[half:, :])


def fold_chunk(kept, arrived, tile):
    rows, width = kept.shape
    half = rows // 2
    spec = lambda n: pl.BlockSpec((n, tile), lambda j: (0, j))
    return pl.pallas_call(
        fold_kernel,
        grid=(width // tile,),
        in_specs=[spec(rows), spec(rows + SCALE_ROWS)],
        out_specs=[spec(half + SCALE_ROWS), spec(half)],
        out_shape=[jax.ShapeDtypeStruct((half + SCALE_ROWS, width), bf16), jax.ShapeDtypeStruct((half, width), f32)],
        compiler_params=params(),
        cost_estimate=pl.CostEstimate(
            flops=20 * rows * width, bytes_accessed=9 * rows * width, transcendentals=2 * rows * width
        ),
        name="fold_chunk",
    )(kept, arrived)


def hidden_kernel(kept, arrived, *refs):
    refs[-1][...] = (kept[...] + get_code(arrived)).astype(bf16)


def hidden_chunk(kept, arrived, before, chunk, tile, columns):
    rows, width = kept.shape
    at = chunk * width // tile
    spec = lambda n: pl.BlockSpec((n, tile), lambda j: (0, j))
    args, in_specs, aliases = [kept, arrived], [spec(rows), spec(rows + SCALE_ROWS)], {}
    if before is not None:
        aliases = {2: 0}
        args.append(before)
        in_specs.append(pl.BlockSpec(memory_space=pl.ANY))
    return pl.pallas_call(
        hidden_kernel,
        grid=(width // tile,),
        in_specs=in_specs,
        out_specs=pl.BlockSpec((rows, tile), lambda j: (0, at + j)),
        out_shape=jax.ShapeDtypeStruct((rows, columns), bf16),
        input_output_aliases=aliases,
        compiler_params=params(),
        cost_estimate=pl.CostEstimate(
            flops=10 * rows * width, bytes_accessed=8 * rows * width, transcendentals=rows * width
        ),
        name="hidden_chunk",
    )(*args)


def exchange_features(both, dp, mp):
    count, tokens, width = both.shape
    inner = mp // dp
    quarter = tokens // dp
    me, outer = lax.axis_index("dp"), lax.axis_index("mp") // inner
    arrived = []
    for k in range(dp):
        pairs = []
        for t in range(dp):
            for o in range(dp):
                for i in range(inner):
                    pairs.append((t * mp + o * inner + i, o * mp + (t ^ k) * inner + i))
        piece = lax.dynamic_slice_in_dim(both, (me ^ k) * quarter, quarter, axis=1)
        arrived.append(lax.ppermute(piece, ("dp", "mp"), pairs))
    arrived = jnp.stack(arrived)
    mine = jnp.stack([lax.dynamic_index_in_dim(arrived, outer ^ me ^ n, 0, keepdims=False) for n in range(dp)])
    return lax.all_gather(mine, "mp", axis=0)


def body(dp, mp, activations, out_grads, weight, row_state, column_state, next_batch):
    rows, columns = weight.shape
    tokens = activations.shape[0] * dp
    inner = mp // dp
    chunks = CHUNKS
    width = columns // chunks
    tile = min(256, width)

    spread = exchange_features(jnp.stack([activations, next_batch]), dp, mp)
    spread = spread.reshape((dp, inner) + spread.shape[1:])
    left = spread[:, :, :, 0].transpose(1, 4, 2, 0, 3).reshape(rows, tokens)
    features = spread[:, :, :, 1].transpose(2, 0, 3, 1, 4).reshape(tokens, rows)

    weight_total = jnp.sum(weight * weight)
    weight_total = all_sum(all_sum(jnp.full((LANES,), weight_total), "mp", mp), "dp", dp)[0]

    before = None
    for c in range(chunks):
        blocks = {0: out_grads[:, c * width : (c + 1) * width]}
        for bit in bit_order(dp, c):
            blocks.update({n ^ bit: swap(blocks[n], "dp", dp, bit) for n in list(blocks)})
        before = gradient_chunk(left, out_grads, [blocks[n] for n in range(1, dp)], before, c, width, tile)
    gradient, row_part, column_part = before

    row_sum = all_sum(jnp.sum(row_part, axis=1), "mp", mp)
    column_sum = all_sum(column_part[0], "dp", dp)
    row_moment = decay_rate * row_state + (1.0 - decay_rate) * (row_sum / (columns * mp))
    column_moment = decay_rate * column_state + (1.0 - decay_rate) * (column_sum / (rows * dp))

    raw_total = jnp.sum(raw_square_sum(gradient, 1.0 / row_moment[:, None], 1.0 / column_moment[None, :], tile))
    raw_total = all_sum(all_sum(jnp.full((LANES,), raw_total), "mp", mp), "dp", dp)[0]
    entries = rows * dp * columns * mp
    rms_update = jnp.sqrt(raw_total / entries)
    rms_weight = jnp.sqrt(weight_total / entries + weight_eps)
    row_scale = lax.rsqrt(row_moment)[:, None]
    column_scale = (lax.rsqrt(column_moment) / jnp.maximum(1.0, rms_update / clip_level))[None, :]
    step = (learn_rate * rms_weight).reshape(1, 1)

    written, hidden = None, None
    pending = []
    for c in range(chunks):
        bits = bit_order(dp, c)
        order = [0]
        for bit in reversed(bits):
            order = order + [n ^ bit for n in order]
        *written, sent, kept = update_chunk(
            gradient, weight, row_scale, column_scale, step, features, written, c, width, tile, order
        )
        pending.append((bits, sent, kept))
    for c, (bits, sent, kept) in enumerate(pending):
        for bit in bits[:-1]:
            sent, kept = fold_chunk(kept, swap(sent, "dp", dp, bit), tile)
        hidden = hidden_chunk(kept, swap(sent, "dp", dp, bits[-1]), hidden, c, tile, columns)
    new_weight, update = written
    return (new_weight, update, row_moment, column_moment, hidden)


def solution(mesh):
    return jax.shard_map(
        functools.partial(body, mesh.shape["dp"], mesh.shape["mp"]),
        mesh=mesh,
        in_specs=(P("dp", "mp"), P("dp", "mp"), P("dp", "mp"), P("dp"), P("mp"), P("dp", "mp")),
        out_specs=(P("dp", "mp"), P("dp", "mp"), P("dp"), P("mp"), P("dp", "mp")),
        check_vma=False,
    )
```

```python
import functools

import jax
import jax.numpy as jnp
from jax import lax
from jax.experimental import pallas as pl
from jax.experimental.pallas import tpu as pltpu
from jax.sharding import PartitionSpec as P

tiny_square = 1e-30
weight_eps = 1e-06
decay_rate = 0.5
clip_level = 0.5
learn_rate = 0.01

f32, bf16 = jnp.float32, jnp.bfloat16
LANES = 128
GRADIENT_SHARES = (3, 3, 3, 3, 2, 2)
UPDATE_SHARES = (1, 1, 2, 2, 3, 3, 2, 2)
SCALE_ROWS = 16
VMEM = 36 * 2**20
SPAN, BASE = 252.0, 125.5


def swap(value, axis, size, bits):
    return lax.ppermute(value, axis, [(i, i ^ bits) for i in range(size)])


def all_sum(value, axis, size):
    bit = 1
    while bit < size:
        value = value + swap(value, axis, size, bit)
        bit *= 2
    return value


def bit_order(dp, chunk):
    bits = [1 << n for n in range(dp.bit_length() - 1)]
    turn = chunk % len(bits)
    return bits[turn:] + bits[:turn]


def params(name=None):
    return pltpu.CompilerParams(vmem_limit_bytes=VMEM)


def encode(values):
    top = jnp.max(jnp.abs(values), axis=0, keepdims=True)
    top = jnp.maximum(top * 1.01, 1e-30).astype(bf16)
    part = jnp.sqrt(jnp.abs(values) * (1.0 / top.astype(f32)))
    size = jnp.exp2(part * SPAN - BASE)
    return jnp.where(values < 0, -size, size).astype(bf16), top


def decode(code, top):
    code = code.astype(f32)
    part = (jnp.log2(jnp.abs(code)) + BASE) * (1.0 / SPAN)
    size = part * part * top.astype(f32)
    return jnp.where(code < 0, -size, size)


def put_code(out_ref, values):
    rows = values.shape[0]
    code, top = encode(values)
    out_ref[0:rows, :] = code
    out_ref[rows : rows + SCALE_ROWS, :] = jnp.broadcast_to(top, (SCALE_ROWS, top.shape[1]))


def get_code(ref):
    rows = ref.shape[0] - SCALE_ROWS
    return decode(ref[0:rows, :], ref[rows : rows + 1, :])


def gradient_kernel(dp, first, *refs):
    left = refs[0]
    blocks = refs[1 : 1 + dp]
    gradient, rows, columns = refs[-3:]
    total = None
    for n in range(dp):
        part = jnp.dot(left[n], blocks[n][...], preferred_element_type=f32)
        total = part if total is None else total + part
    gradient[...] = total
    squares = total * total + tiny_square
    columns[...] = jnp.sum(squares, axis=0, keepdims=True)
    lanes = squares[:, 0:LANES]
    for n in range(1, squares.shape[1] // LANES):
        lanes = lanes + squares[:, n * LANES : (n + 1) * LANES]

    @pl.when(pl.program_id(0) == 0)
    def _():
        rows[...] = lanes if first else refs[1 + dp][...] + lanes

    @pl.when(pl.program_id(0) > 0)
    def _():
        rows[...] += lanes


def gradient_chunk(left, own, near, far, before, start, offset, width, tile):
    dp, rows, depth = left.shape
    tokens, columns = dp * depth, own.shape[1]
    at = start // tile
    whole = lambda shape: pl.BlockSpec(shape, lambda j: (0, 0))
    inside = pl.BlockSpec((depth, tile), lambda j: (0, at + j))
    apart = pl.BlockSpec((depth, tile), lambda j: (0, j))
    shifted = pl.BlockSpec((depth, tile), lambda j: (0, at - offset // tile + j))
    in_specs = [pl.BlockSpec(memory_space=pltpu.VMEM), inside]
    args = [left, own]
    for n in range(1, dp):
        args.append(near[n] if n in near else far[n])
        in_specs.append(shifted if n in near else apart)
    aliases = {}
    if before is not None:
        gradient, row_part, column_part = before
        aliases = {len(args) + 1: 0, len(args) + 2: 2}
        args += [row_part, gradient, column_part]
        in_specs += [whole((rows, LANES)), pl.BlockSpec(memory_space=pl.ANY), pl.BlockSpec(memory_space=pl.ANY)]
    return pl.pallas_call(
        functools.partial(gradient_kernel, dp, before is None),
        grid=(width // tile,),
        in_specs=in_specs,
        out_specs=[
            pl.BlockSpec((rows, tile), lambda j: (0, at + j)),
            whole((rows, LANES)),
            pl.BlockSpec((1, tile), lambda j: (0, at + j)),
        ],
        out_shape=[
            jax.ShapeDtypeStruct((rows, columns), f32),
            jax.ShapeDtypeStruct((rows, LANES), f32),
            jax.ShapeDtypeStruct((1, columns), f32),
        ],
        input_output_aliases=aliases,
        compiler_params=params(),
        cost_estimate=pl.CostEstimate(
            flops=2 * rows * tokens * width, bytes_accessed=4 * rows * width + 2 * tokens * (rows + width), transcendentals=0
        ),
        name="gradient_chunk",
    )(*args)


def update_kernel(order, depth, step, gradient, weight, row_scale, column_scale, features, *refs):
    new_weight, update, sent, kept = refs[-4:]
    change = gradient[...] * row_scale[...] * column_scale[...]
    update[...] = change
    fresh = weight[...] - step[0, 0] * change
    new_weight[...] = fresh
    half = fresh.astype(bf16)
    part_width = features.shape[-1]
    parts = []
    for n in order:
        total = None
        for i in range(features.shape[1]):
            block = features[:, i, n].reshape(depth, part_width)
            part = jnp.dot(block, half[i * part_width : (i + 1) * part_width, :], preferred_element_type=f32)
            total = part if total is None else total + part
        parts.append(total)
    middle = len(order) // 2
    for n in range(middle):
        kept[n * depth : (n + 1) * depth, :] = parts[n]
    put_code(sent, jnp.concatenate(parts[middle:], axis=0))


def update_chunk(gradient, weight, row_scale, column_scale, step, features, before, start, width, tile, order):
    rows, columns = gradient.shape
    depth = features.shape[0] * features.shape[3]
    tokens = depth * len(order)
    at = start // tile
    block = pl.BlockSpec((rows, tile), lambda j: (0, at + j))
    args = [step, gradient, weight, row_scale, column_scale, features]
    in_specs = [
        pl.BlockSpec(memory_space=pltpu.SMEM),
        block,
        block,
        pl.BlockSpec((rows, 1), lambda j: (0, 0)),
        pl.BlockSpec((1, tile), lambda j: (0, at + j)),
        pl.BlockSpec(memory_space=pltpu.VMEM),
    ]
    aliases = {}
    if before is not None:
        aliases = {len(args): 0, len(args) + 1: 1}
        args += list(before)
        in_specs += [pl.BlockSpec(memory_space=pl.ANY)] * 2
    half = tokens // 2
    return pl.pallas_call(
        functools.partial(update_kernel, order, depth),
        grid=(width // tile,),
        in_specs=in_specs,
        out_specs=[
            block,
            block,
            pl.BlockSpec((half + SCALE_ROWS, tile), lambda j: (0, j)),
            pl.BlockSpec((half, tile), lambda j: (0, j)),
        ],
        out_shape=[
            jax.ShapeDtypeStruct((rows, columns), f32),
            jax.ShapeDtypeStruct((rows, columns), f32),
            jax.ShapeDtypeStruct((half + SCALE_ROWS, width), bf16),
            jax.ShapeDtypeStruct((half, width), f32),
        ],
        input_output_aliases=aliases,
        compiler_params=params(),
        cost_estimate=pl.CostEstimate(
            flops=2 * rows * tokens * width,
            bytes_accessed=16 * rows * width + 3 * tokens * width + 2 * tokens * rows,
            transcendentals=tokens * width,
        ),
        name="update_chunk",
    )(*args)


def fold_kernel(kept, arrived, sent, left):
    total = kept[...] + get_code(arrived)
    half = total.shape[0] // 2
    left[...] = total[0:half, :]
    put_code(sent, total[half:, :])


def fold_chunk(kept, arrived, tile):
    rows, width = kept.shape
    half = rows // 2
    spec = lambda n: pl.BlockSpec((n, tile), lambda j: (0, j))
    return pl.pallas_call(
        fold_kernel,
        grid=(width // tile,),
        in_specs=[spec(rows), spec(rows + SCALE_ROWS)],
        out_specs=[spec(half + SCALE_ROWS), spec(half)],
        out_shape=[jax.ShapeDtypeStruct((half + SCALE_ROWS, width), bf16), jax.ShapeDtypeStruct((half, width), f32)],
        compiler_params=params(),
        cost_estimate=pl.CostEstimate(
            flops=20 * rows * width, bytes_accessed=9 * rows * width, transcendentals=2 * rows * width
        ),
        name="fold_chunk",
    )(kept, arrived)


def hidden_kernel(kept, arrived, *refs):
    refs[-1][...] = (kept[...] + get_code(arrived)).astype(bf16)


def hidden_chunk(kept, arrived, before, start, tile, columns):
    rows, width = kept.shape
    at = start // tile
    spec = lambda n: pl.BlockSpec((n, tile), lambda j: (0, j))
    args, in_specs, aliases = [kept, arrived], [spec(rows), spec(rows + SCALE_ROWS)], {}
    if before is not None:
        aliases = {2: 0}
        args.append(before)
        in_specs.append(pl.BlockSpec(memory_space=pl.ANY))
    return pl.pallas_call(
        hidden_kernel,
        grid=(width // tile,),
        in_specs=in_specs,
        out_specs=pl.BlockSpec((rows, tile), lambda j: (0, at + j)),
        out_shape=jax.ShapeDtypeStruct((rows, columns), bf16),
        input_output_aliases=aliases,
        compiler_params=params(),
        cost_estimate=pl.CostEstimate(
            flops=10 * rows * width, bytes_accessed=8 * rows * width, transcendentals=rows * width
        ),
        name="hidden_chunk",
    )(*args)


def turn_features(blocks, dp, mp):
    inner = mp // dp
    me, outer = lax.axis_index("dp"), lax.axis_index("mp") // inner
    quarter = blocks.shape[1] // dp
    pick = lambda k: lax.dynamic_slice_in_dim(blocks, (outer ^ k) * quarter, quarter, axis=1)
    got = jnp.stack([pick(0)] + [swap(pick(k), "mp", mp, k * inner) for k in range(1, dp)])
    pick = lambda n: lax.dynamic_index_in_dim(got, outer ^ me ^ n, 0, keepdims=False)
    return [pick(0)] + [swap(pick(n), "dp", dp, n) for n in range(1, dp)]


def spread_features(block, dp, mp):
    return lax.all_gather(block, "mp", axis=0).reshape((dp, mp // dp) + block.shape)


def cut(columns, shares):
    unit = columns // sum(shares)
    widths = [LANES] * (columns // LANES) if unit % LANES else [unit * n for n in shares]
    return [(sum(widths[:c]), width) for c, width in enumerate(widths)]


class Links:
    def __init__(self, dp):
        self.dp = dp
        self.past = {bit: [] for bit in bit_order(dp, 0)}

    def swap(self, value, bit):
        past = self.past[bit]
        if len(past) >= 2:
            value, _ = lax.optimization_barrier((value, past[-2]))
        past.append(swap(value, "dp", self.dp, bit))
        return past[-1]


def body(dp, mp, activations, out_grads, weight, row_state, column_state, next_batch):
    rows, columns = weight.shape
    links = Links(dp)

    parts = cut(columns, GRADIENT_SHARES)
    edge = parts[2][0]
    ahead, behind = out_grads[:, :edge], out_grads[:, edge:]
    bits = bit_order(dp, 0)
    near_ahead = {bit: swap(ahead, "dp", dp, bit) for bit in bits}
    share = turn_features(jnp.stack([activations, next_batch]), dp, mp)
    share[1], near_ahead, behind = lax.optimization_barrier((share[1], near_ahead, behind))
    share = jnp.stack(share)
    near_behind = {bit: swap(behind, "dp", dp, bit) for bit in bits}
    left = spread_features(share[:, 0], dp, mp)
    features = spread_features(share[:, 1], dp, mp)
    weight_total = jnp.sum(jnp.sum(weight * weight, axis=0))
    left, weight_total = lax.optimization_barrier((left, weight_total))
    left = left.transpose(2, 1, 4, 0, 3).reshape(dp, rows, activations.shape[0])
    left, near_behind = lax.optimization_barrier((left, near_behind))

    tile = min(256, min(width for _, width in parts))
    far = [{} for _ in parts]
    for step in range(1, len(bit_order(dp, 0))):
        for c, (start, width) in enumerate(parts):
            bits = bit_order(dp, c)
            known = [0]
            for bit in bits[:step]:
                known = known + [n ^ bit for n in known]
            for n in known[1:]:
                near, at = (near_ahead, start) if start < edge else (near_behind, start - edge)
                block = far[c][n] if n in far[c] else near[n][:, at : at + width]
                far[c][n ^ bits[step]] = swap(block, "dp", dp, bits[step])
    before = None
    for (start, width), blocks in zip(parts, far):
        near, offset = (near_ahead, 0) if start < edge else (near_behind, edge)
        before = gradient_chunk(left, out_grads, near, blocks, before, start, offset, width, tile)
    gradient, row_part, column_part = before

    row_sum = all_sum(jnp.sum(row_part, axis=1), "mp", mp)
    column_sum = all_sum(column_part[0], "dp", dp)
    row_moment = decay_rate * row_state + (1.0 - decay_rate) * (row_sum / (columns * mp))
    column_moment = decay_rate * column_state + (1.0 - decay_rate) * (column_sum / (rows * dp))

    raw_columns = jnp.sum(gradient * gradient * (1.0 / row_moment)[:, None], axis=0)
    raw_total = jnp.sum(raw_columns / column_moment)
    totals = jnp.where(jnp.arange(LANES) == 0, raw_total, weight_total)
    totals = all_sum(all_sum(totals, "mp", mp), "dp", dp)
    entries = rows * dp * columns * mp
    rms_update = jnp.sqrt(totals[0] / entries)
    rms_weight = jnp.sqrt(totals[1] / entries + weight_eps)
    row_scale = lax.rsqrt(row_moment)[:, None]
    column_scale = (lax.rsqrt(column_moment) / jnp.maximum(1.0, rms_update / clip_level))[None, :]
    step = (learn_rate * rms_weight).reshape(1, 1)

    parts = cut(columns, UPDATE_SHARES)
    tile = min(256, min(width for _, width in parts))
    links = Links(dp)
    written, hidden = None, None
    pending = []
    for c, (start, width) in enumerate(parts):
        bits = bit_order(dp, c)
        order = [0]
        for bit in reversed(bits):
            order = order + [n ^ bit for n in order]
        *written, sent, kept = update_chunk(
            gradient, weight, row_scale, column_scale, step, features, written, start, width, tile, order
        )
        pending.append((kept, links.swap(sent, bits[0])))
    for step in range(1, len(bit_order(dp, 0))):
        for c, (kept, arrived) in enumerate(pending):
            sent, kept = fold_chunk(kept, arrived, tile)
            pending[c] = kept, links.swap(sent, bit_order(dp, c)[step])
    for (start, width), (kept, arrived) in zip(parts, pending):
        hidden = hidden_chunk(kept, arrived, hidden, start, tile, columns)
    new_weight, update = written
    return (new_weight, update, row_moment, column_moment, hidden)


def solution(mesh):
    return jax.shard_map(
        functools.partial(body, mesh.shape["dp"], mesh.shape["mp"]),
        mesh=mesh,
        in_specs=(P("dp", "mp"), P("dp", "mp"), P("dp", "mp"), P("dp"), P("mp"), P("dp", "mp")),
        out_specs=(P("dp", "mp"), P("dp", "mp"), P("dp"), P("mp"), P("dp", "mp")),
        check_vma=False,
    )
```

```python
import functools

import jax
import jax.numpy as jnp
from jax import lax
from jax.experimental import pallas as pl
from jax.experimental.pallas import tpu as pltpu
from jax.sharding import PartitionSpec as P

tiny_square = 1e-30
weight_eps = 1e-06
decay_rate = 0.5
clip_level = 0.5
learn_rate = 0.01

f32, bf16 = jnp.float32, jnp.bfloat16
LANES = 128
GRADIENT_SHARES = (3, 3, 3, 3, 2, 2)
UPDATE_SHARES = (1, 1, 2, 2, 3, 3, 2, 2)
SCALE_ROWS = 16
VMEM = 36 * 2**20
SPAN, BASE = 252.0, 125.5


def swap(value, axis, size, bits):
    return lax.ppermute(value, axis, [(i, i ^ bits) for i in range(size)])


def all_sum(value, axis, size):
    bit = 1
    while bit < size:
        pair = value + swap(value, axis, size, bit)
        if 2 * bit < size:
            pair = pair + (swap(value, axis, size, 2 * bit) + swap(value, axis, size, 3 * bit))
        value = pair
        bit *= 4
    return value


def bit_order(dp, chunk):
    bits = [1 << n for n in range(dp.bit_length() - 1)]
    turn = chunk % len(bits)
    return bits[turn:] + bits[:turn]


def cost(flops, bytes_accessed, transcendentals, share=0.01):
    return pl.CostEstimate(
        flops=int(flops * share),
        bytes_accessed=int(bytes_accessed * share),
        transcendentals=int(transcendentals * share),
    )


def params():
    return pltpu.CompilerParams(vmem_limit_bytes=VMEM)


def encode(values):
    top = jnp.max(jnp.abs(values), axis=0, keepdims=True)
    top = jnp.maximum(top * 1.01, 1e-30).astype(bf16)
    part = jnp.sqrt(jnp.abs(values) * (1.0 / top.astype(f32)))
    size = jnp.exp2(part * SPAN - BASE)
    return jnp.where(values < 0, -size, size).astype(bf16), top


def decode(code, top):
    code = code.astype(f32)
    part = (jnp.log2(jnp.abs(code)) + BASE) * (1.0 / SPAN)
    size = part * part * top.astype(f32)
    return jnp.where(code < 0, -size, size)


def put_code(out_ref, code, top):
    rows = code.shape[0]
    out_ref[0:rows, :] = code
    out_ref[rows : rows + SCALE_ROWS, :] = jnp.broadcast_to(top, (SCALE_ROWS, top.shape[1]))


def get_code(ref):
    rows = ref.shape[0] - SCALE_ROWS
    return decode(ref[0:rows, :], ref[rows : rows + 1, :])


def gradient_kernel(dp, first, *refs):
    left = refs[0]
    blocks = refs[1 : 1 + dp]
    gradient, rows, columns = refs[-3:]
    tokens = jnp.concatenate([block[...] for block in blocks], axis=0)
    total = []
    for i in range(left.shape[1]):
        pieces = [left[o, i, n] for n in range(dp) for o in range(dp)]
        total.append(jnp.dot(jnp.concatenate(pieces, axis=1), tokens, preferred_element_type=f32))
    total = jnp.concatenate(total, axis=0)
    gradient[...] = total
    squares = total * total + tiny_square
    columns[...] = jnp.sum(squares, axis=0, keepdims=True)
    lanes = squares[:, 0:LANES]
    for n in range(1, squares.shape[1] // LANES):
        lanes = lanes + squares[:, n * LANES : (n + 1) * LANES]

    @pl.when(pl.program_id(0) == 0)
    def _():
        rows[...] = lanes if first else refs[1 + dp][...] + lanes

    @pl.when(pl.program_id(0) > 0)
    def _():
        rows[...] += lanes


def gradient_chunk(left, own, near, far, before, start, offset, width):
    dp, inner, _, width_of_part, _ = left.shape
    depth, columns = own.shape
    rows, tokens = inner * width_of_part, dp * depth
    tile = tile_of(start, width)
    at = start // tile
    whole = lambda shape: pl.BlockSpec(shape, lambda j: (0, 0))
    inside = pl.BlockSpec((depth, tile), lambda j: (0, at + j))
    apart = pl.BlockSpec((depth, tile), lambda j: (0, j))
    shifted = pl.BlockSpec((depth, tile), lambda j: (0, (start - offset) // tile + j))
    in_specs = [pl.BlockSpec(memory_space=pltpu.VMEM), inside]
    args = [left, own]
    for n in range(1, dp):
        args.append(near[n] if n in near else far[n])
        in_specs.append(shifted if n in near else apart)
    aliases = {}
    if before is not None:
        gradient, row_part, column_part = before
        aliases = {len(args) + 1: 0, len(args) + 2: 2}
        args += [row_part, gradient, column_part]
        in_specs += [whole((rows, LANES)), pl.BlockSpec(memory_space=pl.ANY), pl.BlockSpec(memory_space=pl.ANY)]
    return pl.pallas_call(
        functools.partial(gradient_kernel, dp, before is None),
        grid=(width // tile,),
        in_specs=in_specs,
        out_specs=[
            pl.BlockSpec((rows, tile), lambda j: (0, at + j)),
            whole((rows, LANES)),
            pl.BlockSpec((1, tile), lambda j: (0, at + j)),
        ],
        out_shape=[
            jax.ShapeDtypeStruct((rows, columns), f32),
            jax.ShapeDtypeStruct((rows, LANES), f32),
            jax.ShapeDtypeStruct((1, columns), f32),
        ],
        input_output_aliases=aliases,
        compiler_params=params(),
        cost_estimate=cost(
            flops=2 * rows * tokens * width, bytes_accessed=4 * rows * width + 2 * tokens * (rows + width), transcendentals=0
        ),
        name="gradient_chunk",
    )(*args)


def update_kernel(orders, steps, step, gradient, weight, row_scale, column_scale, features, *refs):
    members = len(orders)
    new_weight, update = refs[-2 - 2 * members : -2 * members]
    sent, kept = refs[-2 * members : -members], refs[-members:]
    change = gradient[...] * row_scale[...] * column_scale[...]
    update[...] = change
    fresh = weight[...] - step[0, 0] * change
    new_weight[...] = fresh
    half = fresh.astype(bf16)
    member = pl.program_id(0) // steps
    parts = []
    for place in range(len(orders[0])):
        n = orders[0][place]
        for g in range(1, members):
            n = jnp.where(member == g, orders[g][place], n)
        pieces = [features[:, i, n].reshape(-1, features.shape[-1]) for i in range(features.shape[1])]
        parts.append(jnp.dot(jnp.concatenate(pieces, axis=1), half, preferred_element_type=f32))
    middle = len(parts) // 2
    stay = jnp.concatenate(parts[:middle], axis=0)
    code, top = encode(jnp.concatenate(parts[middle:], axis=0))
    for g in range(members):

        @pl.when(member == g)
        def _():
            kept[g][...] = stay
            put_code(sent[g], code, top)


def update_chunks(gradient, weight, row_scale, column_scale, step, features, before, start, width, orders):
    rows, columns = gradient.shape
    depth = features.shape[0] * features.shape[3]
    tokens = depth * len(orders[0])
    tile = tile_of(start, width)
    at, steps, members = start // tile, width // tile, len(orders)
    block = pl.BlockSpec((rows, tile), lambda j: (0, at + j))
    own = lambda height, g: pl.BlockSpec((height, tile), lambda j: (0, jnp.clip(j - g * steps, 0, steps - 1)))
    args = [step, gradient, weight, row_scale, column_scale, features]
    in_specs = [
        pl.BlockSpec(memory_space=pltpu.SMEM),
        block,
        block,
        pl.BlockSpec((rows, 1), lambda j: (0, 0)),
        pl.BlockSpec((1, tile), lambda j: (0, at + j)),
        pl.BlockSpec(memory_space=pltpu.VMEM),
    ]
    aliases = {}
    if before is not None:
        aliases = {len(args): 0, len(args) + 1: 1}
        args += list(before)
        in_specs += [pl.BlockSpec(memory_space=pl.ANY)] * 2
    half = tokens // 2
    out = pl.pallas_call(
        functools.partial(update_kernel, orders, steps),
        grid=(members * steps,),
        in_specs=in_specs,
        out_specs=[block, block]
        + [own(half + SCALE_ROWS, g) for g in range(members)]
        + [own(half, g) for g in range(members)],
        out_shape=[jax.ShapeDtypeStruct((rows, columns), f32)] * 2
        + [jax.ShapeDtypeStruct((half + SCALE_ROWS, width), bf16)] * members
        + [jax.ShapeDtypeStruct((half, width), f32)] * members,
        input_output_aliases=aliases,
        compiler_params=params(),
        cost_estimate=cost(
            flops=2 * rows * tokens * width * members,
            bytes_accessed=(16 * rows * width + 3 * tokens * width) * members + 2 * tokens * rows,
            transcendentals=tokens * width * members,
        ),
        name="update_chunks",
    )(*args)
    return out[:2], out[2 : 2 + members], out[2 + members :]


def fold_kernel(kept, arrived, sent, left):
    total = kept[...] + get_code(arrived)
    half = total.shape[0] // 2
    left[...] = total[0:half, :]
    put_code(sent, *encode(total[half:, :]))


def fold_chunk(kept, arrived):
    rows, width = kept.shape
    tile = tile_of(0, width)
    half = rows // 2
    spec = lambda n: pl.BlockSpec((n, tile), lambda j: (0, j))
    return pl.pallas_call(
        fold_kernel,
        grid=(width // tile,),
        in_specs=[spec(rows), spec(rows + SCALE_ROWS)],
        out_specs=[spec(half + SCALE_ROWS), spec(half)],
        out_shape=[jax.ShapeDtypeStruct((half + SCALE_ROWS, width), bf16), jax.ShapeDtypeStruct((half, width), f32)],
        compiler_params=params(),
        cost_estimate=cost(
            flops=20 * rows * width, bytes_accessed=9 * rows * width, transcendentals=2 * rows * width
        ),
        name="fold_chunk",
    )(kept, arrived)


def hidden_kernel(kept, arrived, *refs):
    refs[-1][...] = (kept[...] + get_code(arrived)).astype(bf16)


def hidden_chunk(kept, arrived, before, start, columns):
    rows, width = kept.shape
    tile = tile_of(start, width)
    at = start // tile
    spec = lambda n: pl.BlockSpec((n, tile), lambda j: (0, j))
    args, in_specs, aliases = [kept, arrived], [spec(rows), spec(rows + SCALE_ROWS)], {}
    if before is not None:
        aliases = {2: 0}
        args.append(before)
        in_specs.append(pl.BlockSpec(memory_space=pl.ANY))
    return pl.pallas_call(
        hidden_kernel,
        grid=(width // tile,),
        in_specs=in_specs,
        out_specs=pl.BlockSpec((rows, tile), lambda j: (0, at + j)),
        out_shape=jax.ShapeDtypeStruct((rows, columns), bf16),
        input_output_aliases=aliases,
        compiler_params=params(),
        cost_estimate=cost(
            flops=10 * rows * width, bytes_accessed=8 * rows * width, transcendentals=rows * width
        ),
        name="hidden_chunk",
    )(*args)


def turn_features(blocks, dp, mp):
    inner = mp // dp
    me, outer = lax.axis_index("dp"), lax.axis_index("mp") // inner
    quarter = blocks.shape[1] // dp
    pick = lambda k: lax.dynamic_slice_in_dim(blocks, (outer ^ k) * quarter, quarter, axis=1)
    got = jnp.stack([pick(0)] + [swap(pick(k), "mp", mp, k * inner) for k in range(1, dp)])
    pick = lambda n: lax.dynamic_index_in_dim(got, outer ^ me ^ n, 0, keepdims=False)
    return [pick(0)] + [swap(pick(n), "dp", dp, n) for n in range(1, dp)]


def spread_features(block, dp, mp):
    return lax.all_gather(block, "mp", axis=0).reshape((dp, mp // dp) + block.shape)


def cut(columns, shares):
    unit = columns // sum(shares)
    widths = [LANES] * (columns // LANES) if unit % LANES else [unit * n for n in shares]
    return [(sum(widths[:c]), width) for c, width in enumerate(widths)]


def tile_of(start, width):
    return 256 if start % 256 == 0 and width % 256 == 0 else LANES


class Links:
    def __init__(self, dp):
        self.dp = dp
        self.past = {bit: [] for bit in bit_order(dp, 0)}

    def swap(self, value, bit):
        past = self.past[bit]
        if len(past) >= 2:
            value, _ = lax.optimization_barrier((value, past[-2]))
        past.append(swap(value, "dp", self.dp, bit))
        return past[-1]


def body(dp, mp, activations, out_grads, weight, row_state, column_state, next_batch):
    rows, columns = weight.shape
    links = Links(dp)

    parts = cut(columns, GRADIENT_SHARES)
    edge = parts[2][0]
    ahead, behind = out_grads[:, :edge], out_grads[:, edge:]
    bits = bit_order(dp, 0)
    near_ahead = {bit: swap(ahead, "dp", dp, bit) for bit in bits}
    share = turn_features(jnp.stack([activations, next_batch]), dp, mp)
    share[1], near_ahead, behind = lax.optimization_barrier((share[1], near_ahead, behind))
    near_behind = {bit: swap(behind, "dp", dp, bit) for bit in bits}
    share = jnp.stack(share)
    left = spread_features(share[:, 0].transpose(0, 2, 1), dp, mp)
    features = spread_features(share[:, 1], dp, mp)
    weight_total = jnp.sum(jnp.sum(weight * weight, axis=0))
    left, weight_total, near_behind = lax.optimization_barrier((left, weight_total, near_behind))

    far = [{} for _ in parts]
    for step in range(1, len(bit_order(dp, 0))):
        for c, (start, width) in enumerate(parts):
            bits = bit_order(dp, c)
            known = [0]
            for bit in bits[:step]:
                known = known + [n ^ bit for n in known]
            for n in known[1:]:
                near, at = (near_ahead, start) if start < edge else (near_behind, start - edge)
                block = far[c][n] if n in far[c] else near[n][:, at : at + width]
                far[c][n ^ bits[step]] = swap(block, "dp", dp, bits[step])
    before = None
    for (start, width), blocks in zip(parts, far):
        near, offset = (near_ahead, 0) if start < edge else (near_behind, edge)
        before = gradient_chunk(left, out_grads, near, blocks, before, start, offset, width)
    gradient, row_part, column_part = before

    row_sum = all_sum(jnp.sum(row_part, axis=1), "mp", mp)
    column_sum = all_sum(column_part[0], "dp", dp)
    row_moment = decay_rate * row_state + (1.0 - decay_rate) * (row_sum / (columns * mp))
    column_moment = decay_rate * column_state + (1.0 - decay_rate) * (column_sum / (rows * dp))

    raw_columns = jnp.sum(gradient * gradient * (1.0 / row_moment)[:, None], axis=0)
    raw_total = jnp.sum(raw_columns / column_moment)
    totals = jnp.where(jnp.arange(LANES) == 0, raw_total, weight_total)
    totals = all_sum(all_sum(totals, "mp", mp), "dp", dp)
    entries = rows * dp * columns * mp
    rms_update = jnp.sqrt(totals[0] / entries)
    rms_weight = jnp.sqrt(totals[1] / entries + weight_eps)
    row_scale = lax.rsqrt(row_moment)[:, None]
    column_scale = (lax.rsqrt(column_moment) / jnp.maximum(1.0, rms_update / clip_level))[None, :]
    step = (learn_rate * rms_weight).reshape(1, 1)

    parts = cut(columns, UPDATE_SHARES)
    links = Links(dp)
    written, hidden = None, None
    pending = []
    ways = len(bit_order(dp, 0))
    for c in range(0, len(parts), ways):
        orders = []
        for member in range(c, min(c + ways, len(parts))):
            order = [0]
            for bit in reversed(bit_order(dp, member)):
                order = order + [n ^ bit for n in order]
            orders.append(order)
        start, width = parts[c]
        written, sent, kept = update_chunks(
            gradient, weight, row_scale, column_scale, step, features, written, start, width, orders
        )
        for g in range(len(orders)):
            pending.append((kept[g], links.swap(sent[g], bit_order(dp, c + g)[0])))
    for step in range(1, len(bit_order(dp, 0))):
        for c, (kept, arrived) in enumerate(pending):
            sent, kept = fold_chunk(kept, arrived)
            pending[c] = kept, links.swap(sent, bit_order(dp, c)[step])
    for (start, width), (kept, arrived) in zip(parts, pending):
        hidden = hidden_chunk(kept, arrived, hidden, start, columns)
    new_weight, update = written
    return (new_weight, update, row_moment, column_moment, hidden)


def solution(mesh):
    return jax.shard_map(
        functools.partial(body, mesh.shape["dp"], mesh.shape["mp"]),
        mesh=mesh,
        in_specs=(P("dp", "mp"), P("dp", "mp"), P("dp", "mp"), P("dp"), P("mp"), P("dp", "mp")),
        out_specs=(P("dp", "mp"), P("dp", "mp"), P("dp"), P("mp"), P("dp", "mp")),
        check_vma=False,
    )
```

```python
import functools

import jax
import jax.numpy as jnp
from jax import lax
from jax.experimental import pallas as pl
from jax.experimental.pallas import tpu as pltpu
from jax.sharding import PartitionSpec as P

tiny_square = 1e-30
weight_eps = 1e-06
decay_rate = 0.5
clip_level = 0.5
learn_rate = 0.01

f32, bf16 = jnp.float32, jnp.bfloat16
LANES = 128
GRADIENT_SHARES = (3, 3, 3, 3, 2, 2)
UPDATE_SHARES = (1, 1, 2, 2, 3, 3, 2, 2)
SCALE_ROWS = 16
VMEM = 36 * 2**20
SPAN, BASE = 252.0, 125.5


def swap(value, axis, size, bits):
    return lax.ppermute(value, axis, [(i, i ^ bits) for i in range(size)])


def all_sum(value, axis, size):
    bit = 1
    while bit < size:
        pair = value + swap(value, axis, size, bit)
        if 2 * bit < size:
            pair = pair + (swap(value, axis, size, 2 * bit) + swap(value, axis, size, 3 * bit))
        value = pair
        bit *= 4
    return value


def bit_order(dp, chunk):
    bits = [1 << n for n in range(dp.bit_length() - 1)]
    turn = chunk % len(bits)
    return bits[turn:] + bits[:turn]


def cost(flops, bytes_accessed, transcendentals, share=0.01):
    return pl.CostEstimate(
        flops=int(flops * share),
        bytes_accessed=int(bytes_accessed * share),
        transcendentals=int(transcendentals * share),
    )


def params():
    return pltpu.CompilerParams(vmem_limit_bytes=VMEM)


def encode(values):
    top = jnp.max(jnp.abs(values), axis=0, keepdims=True)
    top = jnp.maximum(top * 1.01, 1e-30).astype(bf16)
    part = jnp.sqrt(jnp.abs(values) * (1.0 / top.astype(f32)))
    size = jnp.exp2(part * SPAN - BASE)
    return jnp.where(values < 0, -size, size).astype(bf16), top


def decode(code, top):
    code = code.astype(f32)
    part = (jnp.log2(jnp.abs(code)) + BASE) * (1.0 / SPAN)
    size = part * part * top.astype(f32)
    return jnp.where(code < 0, -size, size)


def put_code(out_ref, code, top):
    rows = code.shape[0]
    out_ref[0:rows, :] = code
    out_ref[rows : rows + SCALE_ROWS, :] = jnp.broadcast_to(top, (SCALE_ROWS, top.shape[1]))


def get_code(ref):
    rows = ref.shape[0] - SCALE_ROWS
    return decode(ref[0:rows, :], ref[rows : rows + 1, :])


def gradient_kernel(dp, first, *refs):
    left = refs[0]
    blocks = refs[1 : 1 + dp]
    gradient, rows, columns, short = refs[-4:]
    tokens = jnp.concatenate([block[...] for block in blocks], axis=0)
    total = []
    for i in range(left.shape[1]):
        pieces = [left[o, i, n] for n in range(dp) for o in range(dp)]
        total.append(jnp.dot(jnp.concatenate(pieces, axis=1), tokens, preferred_element_type=f32))
    total = jnp.concatenate(total, axis=0)
    gradient[...] = total
    short[...] = total.astype(bf16)
    squares = total * total + tiny_square
    columns[...] = jnp.sum(squares, axis=0, keepdims=True)
    lanes = squares[:, 0:LANES]
    for n in range(1, squares.shape[1] // LANES):
        lanes = lanes + squares[:, n * LANES : (n + 1) * LANES]

    @pl.when(pl.program_id(0) == 0)
    def _():
        rows[...] = lanes if first else refs[1 + dp][...] + lanes

    @pl.when(pl.program_id(0) > 0)
    def _():
        rows[...] += lanes


def gradient_chunk(left, own, near, far, before, start, offset, width):
    dp, inner, _, width_of_part, _ = left.shape
    depth, columns = own.shape
    rows, tokens = inner * width_of_part, dp * depth
    tile = tile_of(start, width)
    at = start // tile
    whole = lambda shape: pl.BlockSpec(shape, lambda j: (0, 0))
    inside = pl.BlockSpec((depth, tile), lambda j: (0, at + j))
    apart = pl.BlockSpec((depth, tile), lambda j: (0, j))
    shifted = pl.BlockSpec((depth, tile), lambda j: (0, (start - offset) // tile + j))
    in_specs = [pl.BlockSpec(memory_space=pltpu.VMEM), inside]
    args = [left, own]
    for n in range(1, dp):
        args.append(near[n] if n in near else far[n])
        in_specs.append(shifted if n in near else apart)
    aliases = {}
    if before is not None:
        gradient, row_part, column_part, short = before
        aliases = {len(args) + 1: 0, len(args) + 2: 2, len(args) + 3: 3}
        args += [row_part, gradient, column_part, short]
        in_specs += [whole((rows, LANES)), pl.BlockSpec(memory_space=pl.ANY), pl.BlockSpec(memory_space=pl.ANY), pl.BlockSpec(memory_space=pl.ANY)]
    return pl.pallas_call(
        functools.partial(gradient_kernel, dp, before is None),
        grid=(width // tile,),
        in_specs=in_specs,
        out_specs=[
            pl.BlockSpec((rows, tile), lambda j: (0, at + j)),
            whole((rows, LANES)),
            pl.BlockSpec((1, tile), lambda j: (0, at + j)),
            pl.BlockSpec((rows, tile), lambda j: (0, at + j)),
        ],
        out_shape=[
            jax.ShapeDtypeStruct((rows, columns), f32),
            jax.ShapeDtypeStruct((rows, LANES), f32),
            jax.ShapeDtypeStruct((1, columns), f32),
            jax.ShapeDtypeStruct((rows, columns), bf16),
        ],
        input_output_aliases=aliases,
        compiler_params=params(),
        cost_estimate=cost(
            flops=2 * rows * tokens * width, bytes_accessed=4 * rows * width + 2 * tokens * (rows + width), transcendentals=0
        ),
        name="gradient_chunk",
    )(*args)


def update_kernel(orders, steps, step, gradient, weight, row_scale, column_scale, features, *refs):
    members = len(orders)
    new_weight, update = refs[-2 - 2 * members : -2 * members]
    sent, kept = refs[-2 * members : -members], refs[-members:]
    change = gradient[...] * row_scale[...] * column_scale[...]
    update[...] = change
    fresh = weight[...] - step[0, 0] * change
    new_weight[...] = fresh
    half = fresh.astype(bf16)
    member = pl.program_id(0) // steps
    parts = []
    for place in range(len(orders[0])):
        n = orders[0][place]
        for g in range(1, members):
            n = jnp.where(member == g, orders[g][place], n)
        pieces = [features[:, i, n].reshape(-1, features.shape[-1]) for i in range(features.shape[1])]
        parts.append(jnp.dot(jnp.concatenate(pieces, axis=1), half, preferred_element_type=f32))
    middle = len(parts) // 2
    stay = jnp.concatenate(parts[:middle], axis=0)
    code, top = encode(jnp.concatenate(parts[middle:], axis=0))
    for g in range(members):

        @pl.when(member == g)
        def _():
            kept[g][...] = stay
            put_code(sent[g], code, top)


def update_chunks(gradient, weight, row_scale, column_scale, step, features, before, start, width, orders):
    rows, columns = gradient.shape
    depth = features.shape[0] * features.shape[3]
    tokens = depth * len(orders[0])
    tile = tile_of(start, width)
    at, steps, members = start // tile, width // tile, len(orders)
    block = pl.BlockSpec((rows, tile), lambda j: (0, at + j))
    own = lambda height, g: pl.BlockSpec((height, tile), lambda j: (0, jnp.clip(j - g * steps, 0, steps - 1)))
    args = [step, gradient, weight, row_scale, column_scale, features]
    in_specs = [
        pl.BlockSpec(memory_space=pltpu.SMEM),
        block,
        block,
        pl.BlockSpec((rows, 1), lambda j: (0, 0)),
        pl.BlockSpec((1, tile), lambda j: (0, at + j)),
        pl.BlockSpec(memory_space=pltpu.VMEM),
    ]
    aliases = {}
    if before is not None:
        aliases = {len(args): 0, len(args) + 1: 1}
        args += list(before)
        in_specs += [pl.BlockSpec(memory_space=pl.ANY)] * 2
    half = tokens // 2
    out = pl.pallas_call(
        functools.partial(update_kernel, orders, steps),
        grid=(members * steps,),
        in_specs=in_specs,
        out_specs=[block, block]
        + [own(half + SCALE_ROWS, g) for g in range(members)]
        + [own(half, g) for g in range(members)],
        out_shape=[jax.ShapeDtypeStruct((rows, columns), f32)] * 2
        + [jax.ShapeDtypeStruct((half + SCALE_ROWS, width), bf16)] * members
        + [jax.ShapeDtypeStruct((half, width), f32)] * members,
        input_output_aliases=aliases,
        compiler_params=params(),
        cost_estimate=cost(
            flops=2 * rows * tokens * width * members,
            bytes_accessed=(16 * rows * width + 3 * tokens * width) * members + 2 * tokens * rows,
            transcendentals=tokens * width * members,
        ),
        name="update_chunks",
    )(*args)
    return out[:2], out[2 : 2 + members], out[2 + members :]


def fold_kernel(kept, arrived, sent, left):
    total = kept[...] + get_code(arrived)
    half = total.shape[0] // 2
    left[...] = total[0:half, :]
    put_code(sent, *encode(total[half:, :]))


def fold_chunk(kept, arrived):
    rows, width = kept.shape
    tile = tile_of(0, width)
    half = rows // 2
    spec = lambda n: pl.BlockSpec((n, tile), lambda j: (0, j))
    return pl.pallas_call(
        fold_kernel,
        grid=(width // tile,),
        in_specs=[spec(rows), spec(rows + SCALE_ROWS)],
        out_specs=[spec(half + SCALE_ROWS), spec(half)],
        out_shape=[jax.ShapeDtypeStruct((half + SCALE_ROWS, width), bf16), jax.ShapeDtypeStruct((half, width), f32)],
        compiler_params=params(),
        cost_estimate=cost(
            flops=20 * rows * width, bytes_accessed=9 * rows * width, transcendentals=2 * rows * width
        ),
        name="fold_chunk",
    )(kept, arrived)


def hidden_kernel(kept, arrived, *refs):
    refs[-1][...] = (kept[...] + get_code(arrived)).astype(bf16)


def hidden_chunk(kept, arrived, before, start, columns):
    rows, width = kept.shape
    tile = tile_of(start, width)
    at = start // tile
    spec = lambda n: pl.BlockSpec((n, tile), lambda j: (0, j))
    args, in_specs, aliases = [kept, arrived], [spec(rows), spec(rows + SCALE_ROWS)], {}
    if before is not None:
        aliases = {2: 0}
        args.append(before)
        in_specs.append(pl.BlockSpec(memory_space=pl.ANY))
    return pl.pallas_call(
        hidden_kernel,
        grid=(width // tile,),
        in_specs=in_specs,
        out_specs=pl.BlockSpec((rows, tile), lambda j: (0, at + j)),
        out_shape=jax.ShapeDtypeStruct((rows, columns), bf16),
        input_output_aliases=aliases,
        compiler_params=params(),
        cost_estimate=cost(
            flops=10 * rows * width, bytes_accessed=8 * rows * width, transcendentals=rows * width
        ),
        name="hidden_chunk",
    )(*args)


def turn_features(blocks, dp, mp):
    inner = mp // dp
    me, outer = lax.axis_index("dp"), lax.axis_index("mp") // inner
    quarter = blocks.shape[1] // dp
    pick = lambda k: lax.dynamic_slice_in_dim(blocks, (outer ^ k) * quarter, quarter, axis=1)
    got = jnp.stack([pick(0)] + [swap(pick(k), "mp", mp, k * inner) for k in range(1, dp)])
    pick = lambda n: lax.dynamic_index_in_dim(got, outer ^ me ^ n, 0, keepdims=False)
    return [pick(0)] + [swap(pick(n), "dp", dp, n) for n in range(1, dp)]


def spread_features(block, dp, mp):
    return lax.all_gather(block, "mp", axis=0).reshape((dp, mp // dp) + block.shape)


def cut(columns, shares):
    unit = columns // sum(shares)
    widths = [LANES] * (columns // LANES) if unit % LANES else [unit * n for n in shares]
    return [(sum(widths[:c]), width) for c, width in enumerate(widths)]


def tile_of(start, width):
    return 256 if start % 256 == 0 and width % 256 == 0 else LANES


class Links:
    def __init__(self, dp):
        self.dp = dp
        self.past = {bit: [] for bit in bit_order(dp, 0)}

    def swap(self, value, bit):
        past = self.past[bit]
        if len(past) >= 2:
            value, _ = lax.optimization_barrier((value, past[-2]))
        past.append(swap(value, "dp", self.dp, bit))
        return past[-1]


def body(dp, mp, activations, out_grads, weight, row_state, column_state, next_batch):
    rows, columns = weight.shape
    links = Links(dp)

    parts = cut(columns, GRADIENT_SHARES)
    edge = parts[2][0]
    ahead, behind = out_grads[:, :edge], out_grads[:, edge:]
    bits = bit_order(dp, 0)
    near_ahead = {bit: swap(ahead, "dp", dp, bit) for bit in bits}
    share = turn_features(jnp.stack([activations, next_batch]), dp, mp)
    share[1], near_ahead, behind = lax.optimization_barrier((share[1], near_ahead, behind))
    near_behind = {bit: swap(behind, "dp", dp, bit) for bit in bits}
    share = jnp.stack(share)
    left = spread_features(share[:, 0].transpose(0, 2, 1), dp, mp)
    features = spread_features(share[:, 1], dp, mp)
    weight_total = jnp.sum(jnp.sum(weight * weight, axis=0))
    left, weight_total, near_behind = lax.optimization_barrier((left, weight_total, near_behind))

    far = [{} for _ in parts]
    for step in range(1, len(bit_order(dp, 0))):
        for c, (start, width) in enumerate(parts):
            bits = bit_order(dp, c)
            known = [0]
            for bit in bits[:step]:
                known = known + [n ^ bit for n in known]
            for n in known[1:]:
                near, at = (near_ahead, start) if start < edge else (near_behind, start - edge)
                block = far[c][n] if n in far[c] else near[n][:, at : at + width]
                far[c][n ^ bits[step]] = swap(block, "dp", dp, bits[step])
    before = None
    for (start, width), blocks in zip(parts, far):
        near, offset = (near_ahead, 0) if start < edge else (near_behind, edge)
        before = gradient_chunk(left, out_grads, near, blocks, before, start, offset, width)
    gradient, row_part, column_part, short = before

    row_sum = all_sum(jnp.sum(row_part, axis=1), "mp", mp)
    column_sum = all_sum(column_part[0], "dp", dp)
    row_moment = decay_rate * row_state + (1.0 - decay_rate) * (row_sum / (columns * mp))
    column_moment = decay_rate * column_state + (1.0 - decay_rate) * (column_sum / (rows * dp))

    short = short.astype(f32)
    raw_columns = jnp.sum(short * short * (1.0 / row_moment)[:, None], axis=0)
    raw_total = jnp.sum(raw_columns / column_moment)
    totals = jnp.where(jnp.arange(LANES) == 0, raw_total, weight_total)
    totals = all_sum(all_sum(totals, "mp", mp), "dp", dp)
    entries = rows * dp * columns * mp
    rms_update = jnp.sqrt(totals[0] / entries)
    rms_weight = jnp.sqrt(totals[1] / entries + weight_eps)
    row_scale = lax.rsqrt(row_moment)[:, None]
    column_scale = (lax.rsqrt(column_moment) / jnp.maximum(1.0, rms_update / clip_level))[None, :]
    step = (learn_rate * rms_weight).reshape(1, 1)

    parts = cut(columns, UPDATE_SHARES)
    links = Links(dp)
    written, hidden = None, None
    pending = []
    ways = len(bit_order(dp, 0))
    for c in range(0, len(parts), ways):
        orders = []
        for member in range(c, min(c + ways, len(parts))):
            order = [0]
            for bit in reversed(bit_order(dp, member)):
                order = order + [n ^ bit for n in order]
            orders.append(order)
        start, width = parts[c]
        written, sent, kept = update_chunks(
            gradient, weight, row_scale, column_scale, step, features, written, start, width, orders
        )
        for g in range(len(orders)):
            pending.append((kept[g], links.swap(sent[g], bit_order(dp, c + g)[0])))
    for step in range(1, len(bit_order(dp, 0))):
        for c, (kept, arrived) in enumerate(pending):
            sent, kept = fold_chunk(kept, arrived)
            pending[c] = kept, links.swap(sent, bit_order(dp, c)[step])
    for (start, width), (kept, arrived) in zip(parts, pending):
        hidden = hidden_chunk(kept, arrived, hidden, start, columns)
    new_weight, update = written
    return (new_weight, update, row_moment, column_moment, hidden)


def solution(mesh):
    return jax.shard_map(
        functools.partial(body, mesh.shape["dp"], mesh.shape["mp"]),
        mesh=mesh,
        in_specs=(P("dp", "mp"), P("dp", "mp"), P("dp", "mp"), P("dp"), P("mp"), P("dp", "mp")),
        out_specs=(P("dp", "mp"), P("dp", "mp"), P("dp"), P("mp"), P("dp", "mp")),
        check_vma=False,
    )
```
